1024 devices in a mesh: blk: 32 (over z, x_lo), grp: 32 (over x_hi, y, core).
Axes of the slice: x: 4 (x_hi: 2, x_lo: 2; x = x_hi * 2 + x_lo), y: 8, z: 16, core: 2. Of those that a mesh axis runs over, the one named last changes fastest.
Arguments:
- image_embed: bfloat16 [196608, 1152], P(('blk', 'grp')), may hold values from -0.1875 to 0.1875
- text_embed: bfloat16 [196608, 1152], P(('blk', 'grp')), may hold values from -0.1875 to 0.1875
- log_scale: float32 [1], replicated, may hold values from 2.3 to 3
- logit_bias: float32 [1], replicated, may hold values from -3 to -1
Outputs:
- image_grad: float32 [196608, 1152], P(('blk', 'grp'))
- text_grad: float32 [196608, 1152], P(('blk', 'grp'))
- row_loss: float32 [196608], P(('blk', 'grp'))
The draws below stay inside these ranges and needn't reach their ends.
All inputs are finite; a program needn't handle non-finite values.
Results may differ from the reference program's by a relative error of at most 0.005.
Values may be sent and summed in bfloat16 or wider, within the bound.
A program may use at most 32 MiB of HBM per device.

```python
import jax
import jax.numpy as jnp
from jax import lax

D = 1152
R = 192
BLK_STEPS = 2
GRP_STEPS = 4
B = 196608
N_BLK = 32
N_GRP = 32


def block_levels(key, shape, shards, smallest, largest):
    factor_of, own = 1.0, jax.random.fold_in(key, 6)
    for axis_at, blocks in shards:
        draws = jnp.exp(jax.random.uniform(jax.random.fold_in(own, axis_at), (blocks,), jnp.float32, smallest / len(shards), largest / len(shards)))
        factor_of = factor_of * jnp.repeat(draws, shape[axis_at] // blocks).reshape([-1 if axis == axis_at else 1 for axis in range(len(shape))])
    return factor_of


def centred(rng, extent, spread, bound, split=(), kind=jnp.bfloat16):
    level = block_levels(rng, extent, split, -0.22, 0.18) if split else 1.0
    values = jax.random.normal(rng, extent, jnp.float32) * spread * level
    return jnp.minimum(jnp.maximum(values, -bound), bound).astype(kind)


def setup_inputs(seed: int = 0) -> dict:
    seeds = jax.random.split(jax.random.key(seed), 5)
    return {
        "image_embed": centred(seeds[0], (B, D), D ** -0.5, 0.1875, ((0, 1024),)),
        "text_embed": centred(seeds[1], (B, D), D ** -0.5, 0.1875, ((0, 1024),)),
        "log_scale": jnp.clip(jax.random.uniform(seeds[2], (1,), jnp.float32, 2.3, 3.0), 2.3, 3.0),
        "logit_bias": jnp.clip(jax.random.uniform(seeds[3], (1,), jnp.float32, -3.0, -1.0), -3.0, -1.0),
    }


epsilon = 1e-06

def unit_rows(embed):
    values = embed.astype(jnp.float32)
    row_norm = jnp.sqrt(lax.optimization_barrier(jnp.sum(values * values, axis=1, keepdims=True)) + epsilon)
    unit_vec = values / row_norm
    return (row_norm, unit_vec, unit_vec.astype(jnp.bfloat16))

def back_norm(unit_vec, row_norm, hat_grad):
    along = lax.optimization_barrier(jnp.sum(unit_vec * hat_grad, axis=1, keepdims=True))
    return (hat_grad - unit_vec * along) / row_norm

def reference(image_embed, text_embed, log_scale, logit_bias):
    image_norm, image_unit, image_hat = unit_rows(image_embed)
    text_norm, text_unit, text_hat = unit_rows(text_embed)
    factor = jnp.exp(log_scale[0])
    offset_b = logit_bias[0]
    image_f = image_hat.astype(jnp.float32).reshape(N_BLK, N_GRP, R, D)
    text_f = text_hat.astype(jnp.float32).reshape(N_BLK, N_GRP, R, D)
    diag_sign = jnp.where(jnp.eye(R, dtype=bool), 1.0, -1.0).astype(jnp.float32)
    loss_total = jnp.zeros((N_BLK, N_GRP, R), jnp.float32)
    grad_total = jnp.zeros((N_BLK, N_GRP, R, D), jnp.float32)
    text_total = jnp.zeros((N_BLK, N_GRP, R, D), jnp.float32)
    for s in range(BLK_STEPS):
        for t in range(GRP_STEPS):
            block = jnp.roll(text_f, (s, t), axis=(0, 1))
            inner_dot = jnp.einsum('abrd,abnd->abrn', image_f, block, precision=lax.Precision.HIGHEST)
            logits = factor * inner_dot + offset_b
            sign_mat = diag_sign if s == 0 and t == 0 else jnp.float32(-1.0)
            margin = sign_mat * logits
            loss_total = loss_total + lax.optimization_barrier(jnp.sum(jax.nn.softplus(-margin), axis=3))
            slope_w = (factor * -sign_mat * jax.nn.sigmoid(-margin)).astype(jnp.bfloat16).astype(jnp.float32)
            grad_total = grad_total + jnp.einsum('abrn,abnd->abrd', slope_w, block, precision=lax.Precision.HIGHEST)
            piece = jnp.einsum('abrn,abrd->abnd', slope_w, image_f, precision=lax.Precision.HIGHEST)
            text_total = text_total + jnp.roll(piece, (-s, -t), axis=(0, 1))
    image_grad = back_norm(image_unit, image_norm, grad_total.reshape(N_BLK * N_GRP * R, D))
    text_grad = back_norm(text_unit, text_norm, text_total.reshape(N_BLK * N_GRP * R, D))
    row_loss = loss_total.reshape(N_BLK * N_GRP * R) / (BLK_STEPS * GRP_STEPS * R)
    return (image_grad, text_grad, row_loss)
```

```python
import functools

import jax
import jax.numpy as jnp
from jax import lax
from jax.experimental import pallas as pl
from jax.experimental.pallas import tpu as pltpu
from jax.sharding import PartitionSpec as P

MESH = pl.DeviceIdType.MESH
EPS = 1e-06
PAIRS = 8
T1, T2, T3, IM, PA, PB, QS, GS = range(8)


def kernel(n_blk, n_grp, nc, img_ref, txt_ref, scale_ref, bias_ref, ig_ref, tg_ref, loss_ref,
           xs, tb, gi, pt, ra, rb, rq, rgi, s1, s3, sq, sgi, inorm, tnorm, la, ls, lr,
           send_sem, recv_sem, lsend, lrecv):
    blk, grp = lax.axis_index("blk"), lax.axis_index("grp")
    core = lax.rem(grp, 2)
    rows, width = img_ref.shape
    ch = rows // nc
    part = width // 3

    def to(db, dg):
        return (lax.rem(blk + db + n_blk, n_blk), lax.rem(grp + dg + n_grp, n_grp))

    def copy(stream, c, src, dst, target):
        r = pl.ds(c * ch, ch)
        return pltpu.make_async_remote_copy(
            src_ref=src.at[r], dst_ref=dst.at[r],
            send_sem=send_sem.at[stream, c], recv_sem=recv_sem.at[stream, c],
            device_id=target, device_id_type=MESH)

    def got(stream, c, dst):
        copy(stream, c, dst, dst, to(0, 1)).wait_recv()

    def sent(stream, c, src):
        copy(stream, c, src, src, to(0, 1)).wait_send()

    def each(fn):
        for c in range(nc):
            fn(c)

    barrier = pltpu.get_barrier_semaphore()
    for db, dg in ((0, 1), (0, -1), (0, 2), (0, -2), (1, 0), (-1, 0)):
        pl.semaphore_signal(barrier, inc=1, device_id=to(db, dg), device_id_type=MESH)

    def normalize(src, norm, dst):
        def chunk(c, _):
            r = pl.ds(pl.multiple_of(c * 32, 32), 32)
            v = src[r, :].astype(jnp.float32)
            n = jnp.sqrt(jnp.sum(v * v, axis=1, keepdims=True) + EPS)
            norm[r, :] = n
            dst[r, :] = (v / n).astype(jnp.bfloat16)
            return _
        lax.fori_loop(0, rows // 32, chunk, 0)

    normalize(txt_ref, tnorm, tb.at[0])
    normalize(img_ref, inorm, xs.at[0])
    gi[...] = jnp.zeros_like(gi)
    pt[...] = jnp.zeros_like(pt)
    la[...] = jnp.zeros_like(la)
    pl.semaphore_wait(barrier, 6)

    each(lambda c: copy(T2, c, tb.at[0], tb.at[2], to(0, 2)).start())
    each(lambda c: copy(IM, c, xs.at[0], xs.at[1], to(-1, 0)).start())

    @pl.when(core == 0)
    def _():
        each(lambda c: copy(T1, c, tb.at[0], tb.at[1], to(0, 1)).start())

    factor = jnp.exp(jnp.full((1, rows), scale_ref[0], jnp.float32))
    bias = bias_ref[0]

    def compute(which, slot):
        logit = lax.dot_general(tb[slot], xs[which], (((1,), (1,)), ((), ())),
                                preferred_element_type=jnp.float32)
        logit = factor * logit + bias
        own = jnp.logical_and(which == 0, slot == 0)
        at = lax.broadcasted_iota(jnp.int32, (rows, rows), 0)
        to_ = lax.broadcasted_iota(jnp.int32, (rows, rows), 1)
        minus = jnp.where(jnp.logical_and(at == to_, own), -1.0, 1.0).astype(jnp.float32)
        x = minus * logit
        e = jnp.exp(-jnp.abs(x))
        la[which, 0:1, :] += jnp.sum(jnp.maximum(x, 0.0) + jnp.log1p(e), axis=0, keepdims=True)
        slope = (factor * minus * (jnp.where(x >= 0, 1.0, e) / (1.0 + e))).astype(jnp.bfloat16)
        for n in range(3):
            cols = slice(n * part, (n + 1) * part)
            gi[which, :, cols] += lax.dot_general(slope, tb[slot, :, cols], (((0,), (0,)), ((), ())),
                                                  preferred_element_type=jnp.float32)
            pt[slot, :, cols] += jnp.dot(slope, xs[which, :, cols], preferred_element_type=jnp.float32)

    def emit(slot, buf, stream, dst, target):
        for c in range(nc):
            r = pl.ds(c * ch, ch)
            buf[r, :] = pt[slot, r, :].astype(jnp.bfloat16)
            copy(stream, c, buf, dst, target).start()

    def pick(j, values):
        out = jnp.int32(values[-1])
        for i in range(len(values) - 1):
            out = jnp.where(j == i, values[i], out)
        return out

    def step(j, carry):
        c0, c1 = core == 0, core == 1
        at = lambda i0, i1: jnp.logical_or(jnp.logical_and(c0, j == i0), jnp.logical_and(c1, j == i1))

        @pl.when(at(1, 2))
        def _():
            for c in range(nc):
                got(T2, c, tb.at[2])
                copy(T3, c, tb.at[2], tb.at[3], to(0, 1)).start()

                @pl.when(c1)
                def _():
                    copy(T1, c, tb.at[2], tb.at[1], to(0, -1)).start()

        @pl.when(at(2, 1))
        def _():
            each(lambda c: got(T1, c, tb.at[1]))

        @pl.when(at(5, 3))
        def _():
            each(lambda c: got(T3, c, tb.at[3]))

        @pl.when(at(3, 4))
        def _():
            each(lambda c: got(IM, c, xs.at[1]))

        which = jnp.where(c0, pick(j, (0, 0, 0, 1, 1, 0, 1, 1)), pick(j, (0, 0, 0, 0, 1, 1, 1, 1)))
        slot = jnp.where(c0, pick(j, (0, 2, 1, 2, 1, 3, 3, 0)), pick(j, (0, 1, 2, 3, 3, 2, 1, 0)))
        compute(which, slot)

        @pl.when(jnp.logical_and(c0, j == 3))
        def _():
            for c in range(nc):
                r = pl.ds(c * ch, ch)
                got(PB, c, rb)
                sq[r, :] = (pt[2, r, :] + rb[r, :].astype(jnp.float32)).astype(jnp.bfloat16)
                copy(QS, c, sq, rq, to(0, -2)).start()

        @pl.when(jnp.logical_and(c0, j == 4))
        def _():
            emit(1, s1, PB, rb, to(0, 1))

        @pl.when(jnp.logical_and(c0, j == 6))
        def _():
            emit(3, s3, PA, ra, to(0, -1))

        @pl.when(jnp.logical_and(c1, j == 4))
        def _():
            emit(3, s3, PB, rb, to(0, -1))

        @pl.when(jnp.logical_and(c1, j == 6))
        def _():
            emit(1, s1, PA, ra, to(0, -1))
        return carry

    lax.fori_loop(0, 8, step, 0)

    for c in range(nc):
        r = pl.ds(c * ch, ch)
        sgi[r, :] = gi[1, r, :].astype(jnp.bfloat16)
        copy(GS, c, sgi, rgi, to(1, 0)).start()
    ls[...] = la[1]
    lcopy = pltpu.make_async_remote_copy(src_ref=ls, dst_ref=lr, send_sem=lsend, recv_sem=lrecv,
                                         device_id=to(1, 0), device_id_type=MESH)
    lcopy.start()

    @pl.when(core == 1)
    def _():
        for c in range(nc):
            r = pl.ds(c * ch, ch)
            got(PB, c, rb)
            got(PA, c, ra)
            sq[r, :] = (pt[2, r, :] + rb[r, :].astype(jnp.float32)
                        + ra[r, :].astype(jnp.float32)).astype(jnp.bfloat16)
            copy(QS, c, sq, rq, to(0, -2)).start()

    @pl.when(core == 0)
    def _():
        for c in range(nc):
            r = pl.ds(c * ch, ch)
            got(PA, c, ra)
            pt[0, r, :] += ra[r, :].astype(jnp.float32)

    def back(c, src, norm, hat, out):
        r = pl.ds(c * ch, ch)
        n = norm[r, :]
        unit = src[r, :].astype(jnp.float32) / n
        along = jnp.sum(unit * hat, axis=1, keepdims=True)
        out[r, :] = (hat - unit * along) / n

    for c in range(nc):
        r = pl.ds(c * ch, ch)
        got(GS, c, rgi)
        back(c, img_ref, inorm, gi[0, r, :] + rgi[r, :].astype(jnp.float32), ig_ref)
    lcopy.wait()
    loss_ref[...] = (la[0, 0:1, :] + lr[0:1, :]) / (PAIRS * rows)
    for c in range(nc):
        r = pl.ds(c * ch, ch)
        got(QS, c, rq)
        back(c, txt_ref, tnorm, pt[0, r, :] + rq[r, :].astype(jnp.float32), tg_ref)

    for c in range(nc):
        sent(T1, c, tb.at[1])
        sent(T2, c, tb.at[0])
        sent(T3, c, tb.at[2])
        sent(IM, c, xs.at[0])
        sent(PA, c, s1)
        sent(PB, c, s3)
        sent(QS, c, sq)
        sent(GS, c, sgi)


def solution(mesh):
    n_blk, n_grp = mesh.shape["blk"], mesh.shape["grp"]

    def body(image_embed, text_embed, log_scale, logit_bias):
        rows, width = image_embed.shape
        nc = 2
        half = lambda *shape: pltpu.VMEM(shape, jnp.bfloat16)
        full = lambda *shape: pltpu.VMEM(shape, jnp.float32)
        dma = pltpu.SemaphoreType.DMA
        vmem = pl.BlockSpec(memory_space=pltpu.VMEM)
        smem = pl.BlockSpec(memory_space=pltpu.SMEM)
        out = lambda *shape: jax.ShapeDtypeStruct(shape, jnp.float32)
        image_grad, text_grad, loss = pl.pallas_call(
            functools.partial(kernel, n_blk, n_grp, nc),
            out_shape=(out(rows, width), out(rows, width), out(1, rows)),
            in_specs=[vmem, vmem, smem, smem],
            out_specs=(vmem, vmem, vmem),
            scratch_shapes=[
                half(2, rows, width), half(4, rows, width), full(2, rows, width), full(4, rows, width),
                half(rows, width), half(rows, width), half(rows, width), half(rows, width),
                half(rows, width), half(rows, width), half(rows, width), half(rows, width),
                full(rows, 1), full(rows, 1), full(2, 8, rows), full(8, rows), full(8, rows),
                dma((8, nc)), dma((8, nc)), dma, dma,
            ],
            compiler_params=pltpu.CompilerParams(
                collective_id=0, has_side_effects=True, vmem_limit_bytes=40 << 20),
            cost_estimate=pl.CostEstimate(flops=48 * rows * rows * width, bytes_accessed=12 * rows * width,
                                          transcendentals=24 * rows * rows),
            name="band_loss",
        )(image_embed, text_embed, log_scale, logit_bias)
        return image_grad, text_grad, loss.reshape(rows)

    in_specs = (P(("blk", "grp"), None), P(("blk", "grp"), None), P(), P())
    out_specs = (P(("blk", "grp"), None), P(("blk", "grp"), None), P(("blk", "grp")))
    return jax.shard_map(body, mesh=mesh, in_specs=in_specs, out_specs=out_specs, check_vma=False)
```

```python
import functools

import jax
import jax.numpy as jnp
from jax import lax
from jax.experimental import pallas as pl
from jax.experimental.pallas import tpu as pltpu
from jax.sharding import PartitionSpec as P

MESH = pl.DeviceIdType.MESH
EPS = 1e-06
PAIRS = 8
PAD = 256
CHUNKS = 2
T1, T2, T3, IM, PA, PB, PX, QS, GS, U1, U2, U3, F2 = range(13)


def kernel(n_blk, n_grp, nc, img_ref, txt_ref, scale_ref, bias_ref, ig_ref, tg_ref, loss_ref,
           xs, tb, sl, gi, pt, ra, rb, rx, rq, s1, s3, sq, sgi, inorm, tnorm, la, ls, lr,
           send_sem, recv_sem, lsend, lrecv):
    blk, grp = lax.axis_index("blk"), lax.axis_index("grp")
    core = lax.rem(grp, 2)
    rows, width = img_ref.shape
    ch = rows // nc
    part = width // 3
    both = jnp.logical_and
    no = jnp.logical_not
    half = n_grp // 2
    chip = lax.rem(grp, half) // 2
    c0, c1 = core == 0, core == 1
    low, high = chip == 0, chip == half // 2 - 1
    low0, low1, high1 = both(low, c0), both(low, c1), both(high, c1)
    one0, six1 = both(chip == 1, c0), both(chip == half // 2 - 2, c1)
    first, last = blk == 0, blk == n_blk - 1

    def to(db, dg):
        return (lax.rem(blk + db + n_blk, n_blk), lax.rem(grp + dg + 2 * n_grp, n_grp))

    def span(c, base=0):
        if isinstance(c, int):
            return pl.ds(base + c * ch, ch)
        return pl.ds(pl.multiple_of(base + c * ch, 16), ch)

    def copy(stream, c, src, dst, target, send=None, at=0):
        return pltpu.make_async_remote_copy(
            src_ref=src.at[span(c)], dst_ref=dst.at[span(c, at)],
            send_sem=send_sem.at[stream if send is None else send, c], recv_sem=recv_sem.at[stream, c],
            device_id=target, device_id_type=MESH)

    def got(stream, c, dst):
        copy(stream, c, dst, dst, to(0, 1)).wait_recv()

    def sent(stream, c, src):
        copy(stream, c, src, src, to(0, 1)).wait_send()

    def each(fn):
        for c in range(nc):
            fn(c)

    barrier = pltpu.get_barrier_semaphore()

    def greet(*targets):
        for db, dg in targets:
            pl.semaphore_signal(barrier, inc=1, device_id=to(db, dg), device_id_type=MESH)

    greet((0, 1), (0, -1), (0, 2), (0, -2))
    pl.when(no(last))(lambda: greet((1, 0)))
    pl.when(no(first))(lambda: greet((-1, 0)))
    pl.when(low0)(lambda: greet((0, -3)))
    pl.when(high1)(lambda: greet((0, 3)))
    pl.when(one0)(lambda: greet((0, -3)))
    pl.when(six1)(lambda: greet((0, 3)))

    def normalize(src, norm, dst):
        def chunk(c, carry):
            r = pl.ds(pl.multiple_of(c * 32, 32), 32)
            v = src[r, :].astype(jnp.float32)
            n = jnp.sqrt(jnp.sum(v * v, axis=1, keepdims=True) + EPS)
            norm[r, :] = n
            dst[r, :] = (v / n).astype(jnp.bfloat16)
            return carry
        lax.fori_loop(0, rows // 32, chunk, 0)

    normalize(txt_ref, tnorm, tb.at[0])
    normalize(img_ref, inorm, xs)
    xs[rows:PAD, :] = jnp.zeros((PAD - rows, width), jnp.bfloat16)
    xs[PAD + rows:, :] = jnp.zeros((PAD - rows, width), jnp.bfloat16)
    extra = jnp.logical_or(jnp.logical_or(low0, high1), jnp.logical_or(one0, six1))
    pl.semaphore_wait(barrier, jnp.where(first, 5, 6) + jnp.where(extra, 1, 0))
    pl.when(first)(lambda: greet((-1, 0)))
    pl.when(last)(lambda: greet((1, 0)))

    @pl.when(high1)
    def _():
        each(lambda c: copy(T3, c, tb.at[0], tb.at[3], to(0, 3), T2).start())

    @pl.when(no(high))
    def _():
        each(lambda c: copy(T2, c, tb.at[0], tb.at[2], to(0, 2)).start())

    def send_images():
        each(lambda c: copy(IM, c, xs, xs, to(-1, 0), at=PAD).start())

    pl.when(no(first))(send_images)

    @pl.when(c0)
    def _():
        each(lambda c: copy(T1, c, tb.at[0], tb.at[1], to(0, 1)).start())

    @pl.when(last)
    def _():
        each(lambda c: copy(GS, c, tb.at[0], tb.at[4], to(1, 0)).start())

    factor = jnp.exp(jnp.full((1, 1), scale_ref[0], jnp.float32))
    bias = bias_ref[0]
    la[...] = jnp.zeros_like(la)

    def score(text, out, lo, hi, diagonal=False):
        logit = lax.dot_general(text, xs[lo:hi, :], (((1,), (1,)), ((), ())), preferred_element_type=jnp.float32)
        x = factor * logit + bias
        minus = 1.0
        if diagonal:
            at = lax.broadcasted_iota(jnp.int32, x.shape, 0)
            to_ = lax.broadcasted_iota(jnp.int32, x.shape, 1)
            minus = jnp.where(at == to_, -1.0, 1.0).astype(jnp.float32)
            x = minus * x
        e = jnp.exp(-jnp.abs(x))
        la[0:1, lo:hi] += jnp.sum(jnp.maximum(x, 0.0) + jnp.log1p(e), axis=0, keepdims=True)
        slope = factor * minus * (jnp.where(x >= 0, 1.0, e) / (1.0 + e))
        out[...] = slope.astype(jnp.bfloat16)

    def text_part(slot, r):
        for n in range(3):
            cols = slice(n * part, (n + 1) * part)
            pt[slot, r, cols] = jnp.dot(sl[slot, r, :], xs[:, cols], preferred_element_type=jnp.float32)

    def image_part(lo, slot, cols):
        return lax.dot_general(
            sl[slot:slot + 4, :, lo:lo + rows].reshape(4 * rows, rows), tb[slot:slot + 4, :, cols].reshape(4 * rows, part),
            (((0,), (0,)), ((), ())), preferred_element_type=jnp.float32)

    def arrive2(c):
        got(T2, c, tb.at[2])

        @pl.when(no(low1))
        def _():
            copy(T3, c, tb.at[2], tb.at[3], to(0, 1)).start()

        @pl.when(c1)
        def _():
            copy(T1, c, tb.at[2], tb.at[1], to(0, -1)).start()

        @pl.when(both(high, c0))
        def _():
            copy(T2, c, tb.at[0], tb.at[2], to(0, 2)).start()

    def arrive3(c):
        got(T3, c, tb.at[3])

        @pl.when(one0)
        def _():
            copy(T2, c, tb.at[3], tb.at[2], to(0, -1), F2).start()

    every = pl.ds(0, rows)
    score(tb[0], sl.at[0, :, 0:PAD], 0, PAD, True)
    pl.when(no(low))(lambda: each(arrive2))
    pl.when(one0)(lambda: each(arrive3))
    each(lambda c: got(IM, c, xs))

    @pl.when(first)
    def _():
        pl.semaphore_wait(barrier, 1)
        send_images()

    def pick(j, values):
        out = jnp.int32(values[-1])
        for i in range(len(values) - 1):
            out = jnp.where(j == i, values[i], out)
        return out

    def combine(c):
        got(PB, c, rb)
        sq[span(c), :] = (pt[2, span(c), :] + rb[span(c), :].astype(jnp.float32)).astype(jnp.bfloat16)
        copy(QS, c, sq, rq, to(0, -2)).start()

    def meet(slot, r, chunks):
        @pl.when(slot == 1)
        def _():
            for c in chunks:
                got(T1, c, tb.at[1])

        @pl.when(both(slot == 3, no(one0)))
        def _():
            for c in chunks:
                arrive3(c)
        score(tb[slot, r, :], sl.at[slot, r, :], 0, 2 * PAD)
        text_part(slot, r)

        @pl.when(slot == 1)
        def _():
            for c in chunks:
                s1[span(c), :] = pt[1, span(c), :].astype(jnp.bfloat16)
                pl.when(c0)(lambda: copy(PB, c, s1, rb, to(0, 1)).start())
                pl.when(c1)(lambda: copy(PA, c, s1, ra, to(0, -1)).start())

        @pl.when(slot == 3)
        def _():
            for c in chunks:
                s3[span(c), :] = pt[3, span(c), :].astype(jnp.bfloat16)
                pl.when(low0)(lambda: copy(PX, c, s3, rx, to(0, -3)).start())
                pl.when(both(c0, no(low)))(lambda: copy(PA, c, s3, ra, to(0, -1)).start())
                pl.when(c1)(lambda: copy(PB, c, s3, rb, to(0, -1)).start())

        @pl.when(both(c0, jnp.where(low, slot == 1, slot == 2)))
        def _():
            for c in chunks:
                combine(c)

    @pl.when(low)
    def _():
        def step(j, carry):
            slot = jnp.where(c0, pick(lax.rem(j, 3), (2, 3, 1)),
                             jnp.where(j < nc, 1, jnp.where(lax.rem(j - nc, 2) == 0, 3, 2)))
            c = jnp.where(c0, j // 3, jnp.where(j < nc, j, (j - nc) // 2))

            @pl.when(jnp.where(c0, slot == 2, slot == 3))
            def _():
                arrive2(c)
            meet(slot, span(c), (c,))
            return carry
        lax.fori_loop(0, 3 * nc, step, 0)

    @pl.when(no(low))
    def _():
        def step(j, carry):
            meet(jnp.where(c0, pick(j, (2, 1, 3)), pick(j, (3, 2, 1))), every, range(nc))
            return carry
        lax.fori_loop(0, 3, step, 0)

    score(tb[0], sl.at[0, :, PAD:], PAD, 2 * PAD)
    ls[...] = la[:, PAD:]
    lcopy = pltpu.make_async_remote_copy(src_ref=ls, dst_ref=lr, send_sem=lsend, recv_sem=lrecv,
                                         device_id=to(1, 0), device_id_type=MESH)

    @pl.when(no(last))
    def _():
        lcopy.start()
        for n in range(3):
            cols = slice(n * part, (n + 1) * part)
            sgi[:, cols] = image_part(PAD, 0, cols).astype(jnp.bfloat16)
        each(lambda c: copy(GS, c, sgi, tb.at[4], to(1, 0)).start())

    text_part(0, every)
    for n in range(3):
        cols = slice(n * part, (n + 1) * part)
        gi[:, cols] = image_part(0, 0, cols)

    @pl.when(first)
    def _():
        for c in range(nc):
            got(GS, c, tb.at[4])
            copy(U2, c, tb.at[4], tb.at[6], to(0, 2)).start()

            @pl.when(c0)
            def _():
                copy(U1, c, tb.at[4], tb.at[5], to(0, 1)).start()

    @pl.when(c1)
    def _():
        for c in range(nc):
            got(PB, c, rb)
            pt[2, span(c), :] += rb[span(c), :].astype(jnp.float32)

            @pl.when(no(high))
            def _():
                got(PA, c, ra)
                pt[2, span(c), :] += ra[span(c), :].astype(jnp.float32)
            sq[span(c), :] = pt[2, span(c), :].astype(jnp.bfloat16)
            copy(QS, c, sq, rq, to(0, -2)).start()

    @pl.when(first)
    def _():
        for c in range(nc):
            got(U2, c, tb.at[6])
            copy(U3, c, tb.at[6], tb.at[7], to(0, 1)).start()

            @pl.when(c1)
            def _():
                copy(U1, c, tb.at[6], tb.at[5], to(0, -1)).start()

        def seam(j, carry):
            slot = jnp.where(c0, pick(j, (4, 6, 5, 7)), pick(j, (4, 5, 6, 7)))

            @pl.when(slot == 5)
            def _():
                each(lambda c: got(U1, c, tb.at[5]))

            @pl.when(slot == 7)
            def _():
                each(lambda c: got(U3, c, tb.at[7]))
            score(tb[slot], sl.at[slot, :, 0:PAD], 0, PAD)
            return carry
        lax.fori_loop(0, 4, seam, 0)
        for n in range(3):
            cols = slice(n * part, (n + 1) * part)
            gi[:, cols] += image_part(0, 4, cols)
        for c in range(nc):
            sent(U1, c, tb.at[4])
            sent(U2, c, tb.at[4])
            sent(U3, c, tb.at[6])

    @pl.when(c0)
    def _():
        for c in range(nc):
            got(PA, c, ra)
            pt[0, span(c), :] += ra[span(c), :].astype(jnp.float32)

    @pl.when(six1)
    def _():
        for c in range(nc):
            got(PX, c, rx)
            pt[0, span(c), :] += rx[span(c), :].astype(jnp.float32)

    def back(c, src, norm, hat, out):
        n = norm[span(c), :]
        unit = src[span(c), :].astype(jnp.float32) / n
        along = jnp.sum(unit * hat, axis=1, keepdims=True)
        out[span(c), :] = (hat - unit * along) / n

    for c in range(nc):
        @pl.when(no(first))
        def _():
            got(GS, c, tb.at[4])
            gi[span(c), :] += tb[4, span(c), :].astype(jnp.float32)
        back(c, img_ref, inorm, gi[span(c), :], ig_ref)

    @pl.when(no(first))
    def _():
        lcopy.wait_recv()
        la[:, 0:PAD] += lr[...]
    loss_ref[...] = la[0:1, 0:rows] / (PAIRS * rows)
    for c in range(nc):
        got(QS, c, rq)
        back(c, txt_ref, tnorm, pt[0, span(c), :] + rq[span(c), :].astype(jnp.float32), tg_ref)

    for c in range(nc):
        sent(T1, c, tb.at[1])
        sent(IM, c, xs)
        sent(PB, c, s3)
        sent(GS, c, sgi)
        sent(T2, c, tb.at[0])
        sent(QS, c, sq)
        pl.when(one0)(lambda: sent(F2, c, tb.at[3]))
        pl.when(no(low1))(lambda: sent(T3, c, tb.at[2]))

        pl.when(low0)(lambda: sent(PX, c, s3))
        pl.when(no(low0))(lambda: sent(PA, c, s3))

    @pl.when(no(last))
    def _():
        lcopy.wait_send()


def solution(mesh):
    n_blk, n_grp = mesh.shape["blk"], mesh.shape["grp"]

    def body(image_embed, text_embed, log_scale, logit_bias):
        rows, width = image_embed.shape
        nc = CHUNKS
        half = lambda *shape: pltpu.VMEM(shape, jnp.bfloat16)
        full = lambda *shape: pltpu.VMEM(shape, jnp.float32)
        dma = pltpu.SemaphoreType.DMA
        vmem = pl.BlockSpec(memory_space=pltpu.VMEM)
        smem = pl.BlockSpec(memory_space=pltpu.SMEM)
        out = lambda *shape: jax.ShapeDtypeStruct(shape, jnp.float32)
        image_grad, text_grad, loss = pl.pallas_call(
            functools.partial(kernel, n_blk, n_grp, nc),
            out_shape=(out(rows, width), out(rows, width), out(1, rows)),
            in_specs=[vmem, vmem, smem, smem],
            out_specs=(vmem, vmem, vmem),
            scratch_shapes=[
                half(2 * PAD, width), half(8, rows, width), half(8, rows, 2 * PAD), full(rows, width),
                full(4, rows, width), *[half(rows, width)] * 8,
                full(rows, 1), full(rows, 1), full(8, 2 * PAD), full(8, PAD), full(8, PAD),
                dma((13, nc)), dma((12, nc)), dma, dma,
            ],
            compiler_params=pltpu.CompilerParams(
                collective_id=0, has_side_effects=True, vmem_limit_bytes=40 << 20),
            cost_estimate=pl.CostEstimate(flops=48 * rows * rows * width, bytes_accessed=12 * rows * width,
                                          transcendentals=24 * rows * rows),
            name="band_loss",
        )(image_embed, text_embed, log_scale, logit_bias)
        return image_grad, text_grad, loss.reshape(rows)

    in_specs = (P(("blk", "grp"), None), P(("blk", "grp"), None), P(), P())
    out_specs = (P(("blk", "grp"), None), P(("blk", "grp"), None), P(("blk", "grp")))
    return jax.shard_map(body, mesh=mesh, in_specs=in_specs, out_specs=out_specs, check_vma=False)
```

```python
import functools

import jax
import jax.numpy as jnp
from jax import lax
from jax.experimental import pallas as pl
from jax.experimental.pallas import tpu as pltpu
from jax.sharding import PartitionSpec as P

MESH = pl.DeviceIdType.MESH
EPS = 1e-06
PAIRS = 8
PAD = 256
CHUNKS = 2
T1, T2, T3, IM, PA, PB, PX, QS, GS, U1, U2, U3, W2, F2, F4 = range(15)


def kernel(n_blk, n_grp, nc, img_ref, txt_ref, scale_ref, bias_ref, ig_ref, tg_ref, loss_ref,
           xs, tb, sl, gi, pt, ra, rb, rx, rq, s1, s3, sq, sgi, w2, inorm, tnorm, la, ls, lr,
           send_sem, recv_sem, lsend, lrecv):
    blk, grp = lax.axis_index("blk"), lax.axis_index("grp")
    core = lax.rem(grp, 2)
    rows, width = img_ref.shape
    ch = rows // nc
    part = width // 3
    both = jnp.logical_and
    no = jnp.logical_not
    half = n_grp // 2
    chip = lax.rem(grp, half) // 2
    c0, c1 = core == 0, core == 1
    low, high = chip == 0, chip == half // 2 - 1
    low0, low1, high0, high1 = both(low, c0), both(low, c1), both(high, c0), both(high, c1)
    one0, six1 = both(chip == 1, c0), both(chip == half // 2 - 2, c1)
    first, last = blk == 0, blk == n_blk - 1

    def to(db, dg):
        return (lax.rem(blk + db + n_blk, n_blk), lax.rem(grp + dg + 2 * n_grp, n_grp))

    def span(c, base=0):
        if isinstance(c, int):
            return pl.ds(base + c * ch, ch)
        return pl.ds(pl.multiple_of(base + c * ch, 16), ch)

    def copy(stream, c, src, dst, target, send=None, at=0):
        return pltpu.make_async_remote_copy(
            src_ref=src.at[span(c)], dst_ref=dst.at[span(c, at)],
            send_sem=send_sem.at[stream if send is None else send, c], recv_sem=recv_sem.at[stream, c],
            device_id=target, device_id_type=MESH)

    def got(stream, c, dst):
        copy(stream, c, dst, dst, to(0, 1)).wait_recv()

    def sent(stream, c, src):
        copy(stream, c, src, src, to(0, 1)).wait_send()

    def each(fn):
        for c in range(nc):
            fn(c)

    barrier = pltpu.get_barrier_semaphore()

    def greet(*targets):
        for db, dg in targets:
            pl.semaphore_signal(barrier, inc=1, device_id=to(db, dg), device_id_type=MESH)

    greet((0, 1), (0, -1), (0, 2), (0, -2))
    pl.when(no(last))(lambda: greet((1, 0)))
    pl.when(no(first))(lambda: greet((-1, 0)))
    pl.when(low0)(lambda: greet((0, -3), (0, -2 - half)))
    pl.when(high0)(lambda: greet((0, half), (0, 2 + half)))
    pl.when(high1)(lambda: greet((0, 3)))
    pl.when(one0)(lambda: greet((0, -3)))
    pl.when(six1)(lambda: greet((0, 3)))

    def normalize(src, norm, dst):
        def chunk(c, carry):
            r = pl.ds(pl.multiple_of(c * 32, 32), 32)
            v = src[r, :].astype(jnp.float32)
            n = jnp.sqrt(jnp.sum(v * v, axis=1, keepdims=True) + EPS)
            norm[r, :] = n
            dst[r, :] = (v / n).astype(jnp.bfloat16)
            return carry
        lax.fori_loop(0, rows // 32, chunk, 0)

    normalize(txt_ref, tnorm, tb.at[0])
    normalize(img_ref, inorm, xs)
    xs[rows:PAD, :] = jnp.zeros((PAD - rows, width), jnp.bfloat16)
    xs[PAD + rows:, :] = jnp.zeros((PAD - rows, width), jnp.bfloat16)
    extra = jnp.where(jnp.logical_or(low0, high0), 2, jnp.where(jnp.logical_or(high1, jnp.logical_or(one0, six1)), 1, 0))
    pl.semaphore_wait(barrier, jnp.where(first, 5, 6) + extra)
    pl.when(first)(lambda: greet((-1, 0)))
    pl.when(last)(lambda: greet((1, 0)))

    @pl.when(high0)
    def _():
        each(lambda c: copy(W2, c, tb.at[0], w2, to(0, half)).start())

    @pl.when(high1)
    def _():
        each(lambda c: copy(T3, c, tb.at[0], tb.at[3], to(0, 3), T2).start())

    @pl.when(no(high))
    def _():
        each(lambda c: copy(T2, c, tb.at[0], tb.at[2], to(0, 2)).start())

    def send_images():
        each(lambda c: copy(IM, c, xs, xs, to(-1, 0), at=PAD).start())

    def late_images():
        pl.semaphore_wait(barrier, 1)
        send_images()

    pl.when(no(first))(send_images)

    @pl.when(c0)
    def _():
        each(lambda c: copy(T1, c, tb.at[0], tb.at[1], to(0, 1)).start())

    @pl.when(last)
    def _():
        each(lambda c: copy(GS, c, tb.at[0], tb.at[4], to(1, 0)).start())

    factor = jnp.exp(jnp.full((1, 1), scale_ref[0], jnp.float32))
    bias = bias_ref[0]
    la[...] = jnp.zeros_like(la)

    def score(text, out, lo, hi, diagonal=False):
        logit = lax.dot_general(text, xs[lo:hi, :], (((1,), (1,)), ((), ())), preferred_element_type=jnp.float32)
        x = factor * logit + bias
        minus = 1.0
        if diagonal:
            at = lax.broadcasted_iota(jnp.int32, x.shape, 0)
            to_ = lax.broadcasted_iota(jnp.int32, x.shape, 1)
            minus = jnp.where(at == to_, -1.0, 1.0).astype(jnp.float32)
            x = minus * x
        e = jnp.exp(-jnp.abs(x))
        la[0:1, lo:hi] += jnp.sum(jnp.maximum(x, 0.0) + jnp.log1p(e), axis=0, keepdims=True)
        slope = factor * minus * (jnp.where(x >= 0, 1.0, e) / (1.0 + e))
        out[...] = slope.astype(jnp.bfloat16)

    def text_part(slot, r):
        for n in range(3):
            cols = slice(n * part, (n + 1) * part)
            pt[slot, r, cols] = jnp.dot(sl[slot, r, :], xs[:, cols], preferred_element_type=jnp.float32)

    def image_part(lo, slot, cols):
        return lax.dot_general(
            sl[slot:slot + 4, :, lo:lo + rows].reshape(4 * rows, rows), tb[slot:slot + 4, :, cols].reshape(4 * rows, part),
            (((0,), (0,)), ((), ())), preferred_element_type=jnp.float32)

    def arrive2(c):
        got(T2, c, tb.at[2])

        @pl.when(no(low1))
        def _():
            copy(T3, c, tb.at[2], tb.at[3], to(0, 1)).start()

        @pl.when(c1)
        def _():
            copy(T1, c, tb.at[2], tb.at[1], to(0, -1)).start()

        @pl.when(high0)
        def _():
            got(W2, c, w2)
            copy(T2, c, w2, tb.at[2], to(0, 2 + half), F2).start()

    def arrive3(c):
        got(T3, c, tb.at[3])

        @pl.when(one0)
        def _():
            copy(T2, c, tb.at[3], tb.at[2], to(0, -1), F2).start()

    def seam_start():
        for c in range(nc):
            got(GS, c, tb.at[4])

            @pl.when(high1)
            def _():
                copy(U3, c, tb.at[4], tb.at[7], to(0, 3), U2).start()

            @pl.when(no(high1))
            def _():
                copy(U2, c, tb.at[4], tb.at[6], to(0, 2)).start()

            @pl.when(c0)
            def _():
                copy(U1, c, tb.at[4], tb.at[5], to(0, 1)).start()

    every = pl.ds(0, rows)
    score(tb[0], sl.at[0, :, 0:PAD], 0, PAD, True)
    pl.when(no(low))(lambda: each(arrive2))
    pl.when(one0)(lambda: each(arrive3))
    pl.when(both(first, low))(late_images)
    each(lambda c: got(IM, c, xs))

    pl.when(both(first, no(low)))(late_images)

    def pick(j, values):
        out = jnp.int32(values[-1])
        for i in range(len(values) - 1):
            out = jnp.where(j == i, values[i], out)
        return out

    def combine(c):
        got(PB, c, rb)
        sq[span(c), :] = (pt[2, span(c), :] + rb[span(c), :].astype(jnp.float32)).astype(jnp.bfloat16)
        copy(QS, c, sq, rq, to(0, -2)).start()

    def meet(slot, r, chunks):
        @pl.when(slot == 1)
        def _():
            for c in chunks:
                got(T1, c, tb.at[1])

        @pl.when(both(slot == 3, no(one0)))
        def _():
            for c in chunks:
                arrive3(c)
        score(tb[slot, r, :], sl.at[slot, r, :], 0, 2 * PAD)
        text_part(slot, r)

        @pl.when(slot == 1)
        def _():
            for c in chunks:
                s1[span(c), :] = pt[1, span(c), :].astype(jnp.bfloat16)
                pl.when(c0)(lambda: copy(PB, c, s1, rb, to(0, 1)).start())
                pl.when(c1)(lambda: copy(PA, c, s1, ra, to(0, -1)).start())

        @pl.when(slot == 3)
        def _():
            for c in chunks:
                s3[span(c), :] = pt[3, span(c), :].astype(jnp.bfloat16)
                pl.when(low0)(lambda: copy(PX, c, s3, rx, to(0, -3)).start())
                pl.when(both(c0, no(low)))(lambda: copy(PA, c, s3, ra, to(0, -1)).start())
                pl.when(c1)(lambda: copy(PB, c, s3, rb, to(0, -1)).start())

        @pl.when(both(c0, jnp.where(low, slot == 1, slot == 2)))
        def _():
            for c in chunks:
                combine(c)

    @pl.when(low)
    def _():
        def step(j, carry):
            slot = jnp.where(c0, pick(lax.rem(j, 3), (2, 3, 1)),
                             jnp.where(j < nc, 1, jnp.where(lax.rem(j - nc, 2) == 0, 3, 2)))
            c = jnp.where(c0, j // 3, jnp.where(j < nc, j, (j - nc) // 2))

            @pl.when(jnp.where(c0, slot == 2, slot == 3))
            def _():
                arrive2(c)
            meet(slot, span(c), (c,))
            return carry
        lax.fori_loop(0, 3 * nc, step, 0)

    @pl.when(no(low))
    def _():
        def step(j, carry):
            meet(jnp.where(c0, pick(j, (2, 1, 3)), pick(j, (3, 2, 1))), every, range(nc))
            return carry
        lax.fori_loop(0, 3, step, 0)

    pl.when(both(first, low))(seam_start)
    score(tb[0], sl.at[0, :, PAD:], PAD, 2 * PAD)
    ls[...] = la[:, PAD:]
    lcopy = pltpu.make_async_remote_copy(src_ref=ls, dst_ref=lr, send_sem=lsend, recv_sem=lrecv,
                                         device_id=to(1, 0), device_id_type=MESH)

    @pl.when(no(last))
    def _():
        lcopy.start()
        for n in range(3):
            cols = slice(n * part, (n + 1) * part)
            sgi[:, cols] = image_part(PAD, 0, cols).astype(jnp.bfloat16)
        each(lambda c: copy(GS, c, sgi, tb.at[4], to(1, 0)).start())

    text_part(0, every)
    for n in range(3):
        cols = slice(n * part, (n + 1) * part)
        gi[:, cols] = image_part(0, 0, cols)

    pl.when(both(first, no(low)))(seam_start)

    @pl.when(c1)
    def _():
        for c in range(nc):
            got(PB, c, rb)
            pt[2, span(c), :] += rb[span(c), :].astype(jnp.float32)

            @pl.when(no(high))
            def _():
                got(PA, c, ra)
                pt[2, span(c), :] += ra[span(c), :].astype(jnp.float32)
            sq[span(c), :] = pt[2, span(c), :].astype(jnp.bfloat16)
            copy(QS, c, sq, rq, to(0, -2)).start()

    @pl.when(first)
    def _():
        for c in range(nc):
            @pl.when(one0)
            def _():
                got(U3, c, tb.at[7])
                copy(U2, c, tb.at[7], tb.at[6], to(0, -1), F4).start()
            got(U2, c, tb.at[6])

            @pl.when(no(low1))
            def _():
                copy(U3, c, tb.at[6], tb.at[7], to(0, 1)).start()

            @pl.when(c1)
            def _():
                copy(U1, c, tb.at[6], tb.at[5], to(0, -1)).start()

        def seam(j, carry):
            slot = jnp.where(c0, pick(j, (4, 6, 5, 7)), pick(j, (4, 5, 6, 7)))

            @pl.when(slot == 5)
            def _():
                each(lambda c: got(U1, c, tb.at[5]))

            @pl.when(both(slot == 7, no(one0)))
            def _():
                each(lambda c: got(U3, c, tb.at[7]))
            score(tb[slot], sl.at[slot, :, 0:PAD], 0, PAD)
            return carry
        lax.fori_loop(0, 4, seam, 0)
        for n in range(3):
            cols = slice(n * part, (n + 1) * part)
            gi[:, cols] += image_part(0, 4, cols)
        for c in range(nc):
            sent(U1, c, tb.at[4])
            sent(U2, c, tb.at[4])
            pl.when(no(low1))(lambda: sent(U3, c, tb.at[6]))
            pl.when(one0)(lambda: sent(F4, c, tb.at[7]))

    @pl.when(c0)
    def _():
        for c in range(nc):
            got(PA, c, ra)
            pt[0, span(c), :] += ra[span(c), :].astype(jnp.float32)

    @pl.when(six1)
    def _():
        for c in range(nc):
            got(PX, c, rx)
            pt[0, span(c), :] += rx[span(c), :].astype(jnp.float32)

    def back(c, src, norm, hat, out):
        n = norm[span(c), :]
        unit = src[span(c), :].astype(jnp.float32) / n
        along = jnp.sum(unit * hat, axis=1, keepdims=True)
        out[span(c), :] = (hat - unit * along) / n

    for c in range(nc):
        @pl.when(no(first))
        def _():
            got(GS, c, tb.at[4])
            gi[span(c), :] += tb[4, span(c), :].astype(jnp.float32)
        back(c, img_ref, inorm, gi[span(c), :], ig_ref)

    @pl.when(no(first))
    def _():
        lcopy.wait_recv()
        la[:, 0:PAD] += lr[...]
    loss_ref[...] = la[0:1, 0:rows] / (PAIRS * rows)
    for c in range(nc):
        got(QS, c, rq)
        back(c, txt_ref, tnorm, pt[0, span(c), :] + rq[span(c), :].astype(jnp.float32), tg_ref)

    for c in range(nc):
        sent(T1, c, tb.at[1])
        sent(IM, c, xs)
        sent(PB, c, s3)
        sent(GS, c, sgi)
        pl.when(high0)(lambda: sent(W2, c, tb.at[0]))
        pl.when(no(high0))(lambda: sent(T2, c, tb.at[0]))
        sent(QS, c, sq)
        pl.when(jnp.logical_or(one0, high0))(lambda: sent(F2, c, tb.at[3]))
        pl.when(no(low1))(lambda: sent(T3, c, tb.at[2]))

        pl.when(low0)(lambda: sent(PX, c, s3))
        pl.when(no(low0))(lambda: sent(PA, c, s3))

    @pl.when(no(last))
    def _():
        lcopy.wait_send()


def solution(mesh):
    n_blk, n_grp = mesh.shape["blk"], mesh.shape["grp"]

    def body(image_embed, text_embed, log_scale, logit_bias):
        rows, width = image_embed.shape
        nc = CHUNKS
        half = lambda *shape: pltpu.VMEM(shape, jnp.bfloat16)
        full = lambda *shape: pltpu.VMEM(shape, jnp.float32)
        dma = pltpu.SemaphoreType.DMA
        vmem = pl.BlockSpec(memory_space=pltpu.VMEM)
        smem = pl.BlockSpec(memory_space=pltpu.SMEM)
        out = lambda *shape: jax.ShapeDtypeStruct(shape, jnp.float32)
        image_grad, text_grad, loss = pl.pallas_call(
            functools.partial(kernel, n_blk, n_grp, nc),
            out_shape=(out(rows, width), out(rows, width), out(1, rows)),
            in_specs=[vmem, vmem, smem, smem],
            out_specs=(vmem, vmem, vmem),
            scratch_shapes=[
                half(2 * PAD, width), half(8, rows, width), half(8, rows, 2 * PAD), full(rows, width),
                full(4, rows, width), *[half(rows, width)] * 9,
                full(rows, 1), full(rows, 1), full(8, 2 * PAD), full(8, PAD), full(8, PAD),
                dma((15, nc)), dma((13, nc)), dma, dma,
            ],
            compiler_params=pltpu.CompilerParams(
                collective_id=0, has_side_effects=True, vmem_limit_bytes=40 << 20),
            cost_estimate=pl.CostEstimate(flops=48 * rows * rows * width, bytes_accessed=12 * rows * width,
                                          transcendentals=24 * rows * rows),
            name="band_loss",
        )(image_embed, text_embed, log_scale, logit_bias)
        return image_grad, text_grad, loss.reshape(rows)

    in_specs = (P(("blk", "grp"), None), P(("blk", "grp"), None), P(), P())
    out_specs = (P(("blk", "grp"), None), P(("blk", "grp"), None), P(("blk", "grp")))
    return jax.shard_map(body, mesh=mesh, in_specs=in_specs, out_specs=out_specs, check_vma=False)
```

```python
import functools

import jax
import jax.numpy as jnp
from jax import lax
from jax.experimental import pallas as pl
from jax.experimental.pallas import tpu as pltpu
from jax.sharding import PartitionSpec as P

MESH = pl.DeviceIdType.MESH
EPS = 1e-06
PAIRS = 8
PAD = 256
CHUNKS = 2
T1, T2, T3, IM, PA, PB, PX, QS, GS, U1, U2, U3, W2, F2, F4 = range(15)


def kernel(n_blk, n_grp, nc, img_ref, txt_ref, scale_ref, bias_ref, ig_ref, tg_ref, loss_ref,
           xs, tb, sl, gi, pt, ra, rb, rx, rq, s1, s3, sq, sgi, w2, inorm, tnorm, la, ls, lr,
           send_sem, recv_sem, lsend, lrecv):
    blk, grp = lax.axis_index("blk"), lax.axis_index("grp")
    core = lax.rem(grp, 2)
    rows, width = img_ref.shape
    ch = rows // nc
    part = width // 3
    both = jnp.logical_and
    no = jnp.logical_not
    half = n_grp // 2
    chip = lax.rem(grp, half) // 2
    c0, c1 = core == 0, core == 1
    low, high = chip == 0, chip == half // 2 - 1
    low0, low1, high0, high1 = both(low, c0), both(low, c1), both(high, c0), both(high, c1)
    one0, six1 = both(chip == 1, c0), both(chip == half // 2 - 2, c1)
    first, last = blk == 0, blk == n_blk - 1
    origin = both(first, grp == 0)
    near = functools.reduce(jnp.logical_or, [grp == k for k in (1, 2, half - 2, n_grp - 2, n_grp - 1)])
    near = both(first, near)
    near_blk, near_six = both(blk == 1, grp == 0), both(first, grp == n_grp - 3)

    def to(db, dg):
        return (lax.rem(blk + db + n_blk, n_blk), lax.rem(grp + dg + 2 * n_grp, n_grp))

    def span(c, base=0):
        if isinstance(c, int):
            return pl.ds(base + c * ch, ch)
        return pl.ds(pl.multiple_of(base + c * ch, 16), ch)

    def copy(stream, c, src, dst, target, send=None, at=0):
        return pltpu.make_async_remote_copy(
            src_ref=src.at[span(c)], dst_ref=dst.at[span(c, at)],
            send_sem=send_sem.at[stream if send is None else send, c], recv_sem=recv_sem.at[stream, c],
            device_id=target, device_id_type=MESH)

    def got(stream, c, dst):
        copy(stream, c, dst, dst, to(0, 1)).wait_recv()

    def sent(stream, c, src):
        copy(stream, c, src, src, to(0, 1)).wait_send()

    def each(fn):
        for c in range(nc):
            fn(c)

    barrier = pltpu.get_barrier_semaphore()

    def greet(*targets):
        for db, dg in targets:
            pl.semaphore_signal(barrier, inc=1, device_id=to(db, dg), device_id_type=MESH)

    early = no(origin)
    for step_ in (1, -1, 2, -2):
        pl.when(both(early, no(both(first, lax.rem(grp + step_ + n_grp, n_grp) == 0))))(
            functools.partial(greet, (0, step_)))
    pl.when(both(early, no(last)))(lambda: greet((1, 0)))
    pl.when(no(jnp.logical_or(first, near_blk)))(lambda: greet((-1, 0)))
    pl.when(both(early, low0))(lambda: greet((0, -3), (0, -2 - half)))
    pl.when(high0)(lambda: greet((0, half)))
    pl.when(both(high0, no(near)))(lambda: greet((0, 2 + half)))
    pl.when(both(high0, both(near, grp != half - 2)))(lambda: greet((0, 2 + half)))
    pl.when(high1)(lambda: greet((0, 3)))
    pl.when(one0)(lambda: greet((0, -3)))
    pl.when(both(six1, no(near_six)))(lambda: greet((0, 3)))

    def normalize(src, norm, dst):
        def chunk(c, carry):
            r = pl.ds(pl.multiple_of(c * 32, 32), 32)
            v = src[r, :].astype(jnp.float32)
            n = jnp.sqrt(jnp.sum(v * v, axis=1, keepdims=True) + EPS)
            norm[r, :] = n
            dst[r, :] = (v / n).astype(jnp.bfloat16)
            return carry
        lax.fori_loop(0, rows // 32, chunk, 0)

    normalize(txt_ref, tnorm, tb.at[0])
    normalize(img_ref, inorm, xs)
    xs[rows:PAD, :] = jnp.zeros((PAD - rows, width), jnp.bfloat16)
    xs[PAD + rows:, :] = jnp.zeros((PAD - rows, width), jnp.bfloat16)
    extra = jnp.where(jnp.logical_or(low0, high0), 2, jnp.where(jnp.logical_or(high1, jnp.logical_or(one0, six1)), 1, 0))
    fewer = jnp.where(jnp.logical_or(near, jnp.logical_or(near_blk, near_six)), 1, 0)
    pl.semaphore_wait(barrier, jnp.where(first, 5, 6) + extra - fewer)
    pl.when(first)(lambda: greet((-1, 0)))
    pl.when(last)(lambda: greet((1, 0)))
    pl.when(jnp.logical_or(near, near_six))(lambda: greet((0, n_grp - grp)))
    pl.when(near_blk)(lambda: greet((-1, 0)))
    pl.when(origin)(lambda: greet((0, 1), (0, -1), (0, 2), (0, -2), (0, half - 2), (1, 0)))

    @pl.when(high0)
    def _():
        each(lambda c: copy(W2, c, tb.at[0], w2, to(0, half)).start())

    @pl.when(high1)
    def _():
        each(lambda c: copy(T3, c, tb.at[0], tb.at[3], to(0, 3), T2).start())

    @pl.when(no(high))
    def _():
        each(lambda c: copy(T2, c, tb.at[0], tb.at[2], to(0, 2)).start())

    def send_images():
        each(lambda c: copy(IM, c, xs, xs, to(-1, 0), at=PAD).start())

    def late_images():
        pl.semaphore_wait(barrier, jnp.where(near, 2, 1))
        send_images()

    pl.when(no(jnp.logical_or(first, near_blk)))(send_images)

    @pl.when(c0)
    def _():
        each(lambda c: copy(T1, c, tb.at[0], tb.at[1], to(0, 1)).start())

    def send_seam(c):
        copy(GS, c, tb.at[0], tb.at[4], to(1, 0)).start()

    pl.when(both(last, low))(lambda: send_seam(0))
    pl.when(both(last, no(low)))(lambda: each(send_seam))

    factor = jnp.exp(jnp.full((1, 1), scale_ref[0], jnp.float32))
    bias = bias_ref[0]
    la[...] = jnp.zeros_like(la)

    def score(text, out, lo, hi, diagonal=False):
        logit = lax.dot_general(text, xs[lo:hi, :], (((1,), (1,)), ((), ())), preferred_element_type=jnp.float32)
        x = factor * logit + bias
        minus = 1.0
        if diagonal:
            at = lax.broadcasted_iota(jnp.int32, x.shape, 0)
            to_ = lax.broadcasted_iota(jnp.int32, x.shape, 1)
            minus = jnp.where(at == to_, -1.0, 1.0).astype(jnp.float32)
            x = minus * x
        e = jnp.exp(-jnp.abs(x))
        la[0:1, lo:hi] += jnp.sum(jnp.maximum(x, 0.0) + jnp.log1p(e), axis=0, keepdims=True)
        slope = factor * minus * (jnp.where(x >= 0, 1.0, e) / (1.0 + e))
        out[...] = slope.astype(jnp.bfloat16)

    def text_part(slot, r):
        for n in range(3):
            cols = slice(n * part, (n + 1) * part)
            pt[slot, r, cols] = jnp.dot(sl[slot, r, :], xs[:, cols], preferred_element_type=jnp.float32)

    def image_part(lo, slot, cols):
        return lax.dot_general(
            sl[slot:slot + 4, :, lo:lo + rows].reshape(4 * rows, rows), tb[slot:slot + 4, :, cols].reshape(4 * rows, part),
            (((0,), (0,)), ((), ())), preferred_element_type=jnp.float32)

    def arrive2(c):
        got(T2, c, tb.at[2])

        @pl.when(no(jnp.logical_or(low1, both(near, high1))))
        def _():
            copy(T3, c, tb.at[2], tb.at[3], to(0, 1)).start()

        @pl.when(c1)
        def _():
            copy(T1, c, tb.at[2], tb.at[1], to(0, -1)).start()

    def arrive3(c):
        got(T3, c, tb.at[3])

        @pl.when(one0)
        def _():
            copy(T2, c, tb.at[3], tb.at[2], to(0, -1), F2).start()

    def seam_chunk(c):
        got(GS, c, tb.at[4])

        @pl.when(high1)
        def _():
            copy(U3, c, tb.at[4], tb.at[7], to(0, 3), U2).start()

        @pl.when(no(high1))
        def _():
            copy(U2, c, tb.at[4], tb.at[6], to(0, 2)).start()

        @pl.when(c0)
        def _():
            copy(U1, c, tb.at[4], tb.at[5], to(0, 1)).start()

    def seam_start():
        each(seam_chunk)

    every = pl.ds(0, rows)
    score(tb[0], sl.at[0, :, 0:PAD], 0, PAD, True)
    pl.when(no(low))(lambda: each(arrive2))

    def relay():
        for c in range(nc):
            got(W2, c, w2)
            copy(T2, c, w2, tb.at[2], to(0, 2 + half), F2).start()

    before_origin = both(first, grp == half - 2)
    pl.when(both(high0, no(before_origin)))(relay)
    pl.when(one0)(lambda: each(arrive3))
    pl.when(jnp.logical_or(both(near, low), near_blk))(late_images)
    got(IM, 0, xs)

    @pl.when(both(last, low))
    def _():
        for c in range(1, nc):
            send_seam(c)
    for c in range(1, nc):
        got(IM, c, xs)

    pl.when(both(first, no(low)))(late_images)
    pl.when(before_origin)(relay)

    @pl.when(both(high1, near))
    def _():
        each(lambda c: copy(T3, c, tb.at[2], tb.at[3], to(0, 1)).start())

    def pick(j, values):
        out = jnp.int32(values[-1])
        for i in range(len(values) - 1):
            out = jnp.where(j == i, values[i], out)
        return out

    def combine(c):
        got(PB, c, rb)
        sq[span(c), :] = (pt[2, span(c), :] + rb[span(c), :].astype(jnp.float32)).astype(jnp.bfloat16)
        copy(QS, c, sq, rq, to(0, -2)).start()

    def meet(slot, r, chunks):
        @pl.when(slot == 1)
        def _():
            for c in chunks:
                got(T1, c, tb.at[1])

        @pl.when(both(slot == 3, no(one0)))
        def _():
            for c in chunks:
                arrive3(c)
        score(tb[slot, r, :], sl.at[slot, r, :], 0, 2 * PAD)
        text_part(slot, r)

        @pl.when(slot == 1)
        def _():
            for c in chunks:
                s1[span(c), :] = pt[1, span(c), :].astype(jnp.bfloat16)
                pl.when(c0)(lambda: copy(PB, c, s1, rb, to(0, 1)).start())
                pl.when(c1)(lambda: copy(PA, c, s1, ra, to(0, -1)).start())

        @pl.when(slot == 3)
        def _():
            for c in chunks:
                s3[span(c), :] = pt[3, span(c), :].astype(jnp.bfloat16)
                pl.when(low0)(lambda: copy(PX, c, s3, rx, to(0, -3)).start())
                pl.when(both(c0, no(low)))(lambda: copy(PA, c, s3, ra, to(0, -1)).start())
                pl.when(c1)(lambda: copy(PB, c, s3, rb, to(0, -1)).start())

        @pl.when(both(c0, jnp.where(low, slot == 1, slot == 2)))
        def _():
            for c in chunks:
                combine(c)

    @pl.when(low)
    def _():
        def step(j, carry):
            slot = jnp.where(c0, pick(lax.rem(j, 3), (2, 3, 1)),
                             jnp.where(j < nc, 1, jnp.where(lax.rem(j - nc, 2) == 0, 3, 2)))
            c = jnp.where(c0, j // 3, jnp.where(j < nc, j, (j - nc) // 2))

            @pl.when(jnp.where(c0, slot == 2, slot == 3))
            def _():
                arrive2(c)
            meet(slot, span(c), (c,))
            pl.when(both(both(first, no(near)), j == 1))(late_images)

            for k in range(nc):
                pl.when(both(first, j == 2 + 3 * k))(functools.partial(seam_chunk, k))
            return carry
        lax.fori_loop(0, 3 * nc, step, 0)

    @pl.when(no(low))
    def _():
        def step(j, carry):
            meet(jnp.where(c0, pick(j, (2, 1, 3)), pick(j, (3, 2, 1))), every, range(nc))
            return carry
        lax.fori_loop(0, 3, step, 0)

    score(tb[0], sl.at[0, :, PAD:], PAD, 2 * PAD)
    ls[...] = la[:, PAD:]
    lcopy = pltpu.make_async_remote_copy(src_ref=ls, dst_ref=lr, send_sem=lsend, recv_sem=lrecv,
                                         device_id=to(1, 0), device_id_type=MESH)

    @pl.when(no(last))
    def _():
        lcopy.start()
        for n in range(3):
            cols = slice(n * part, (n + 1) * part)
            sgi[:, cols] = image_part(PAD, 0, cols).astype(jnp.bfloat16)
        each(lambda c: copy(GS, c, sgi, tb.at[4], to(1, 0)).start())

    text_part(0, every)
    for n in range(3):
        cols = slice(n * part, (n + 1) * part)
        gi[:, cols] = image_part(0, 0, cols)

    pl.when(both(first, no(low)))(seam_start)

    @pl.when(c1)
    def _():
        for c in range(nc):
            got(PB, c, rb)
            pt[2, span(c), :] += rb[span(c), :].astype(jnp.float32)

            @pl.when(no(high))
            def _():
                got(PA, c, ra)
                pt[2, span(c), :] += ra[span(c), :].astype(jnp.float32)
            sq[span(c), :] = pt[2, span(c), :].astype(jnp.bfloat16)
            copy(QS, c, sq, rq, to(0, -2)).start()

    @pl.when(both(first, one0))
    def _():
        for c in range(nc):
            got(U3, c, tb.at[7])
            copy(U2, c, tb.at[7], tb.at[6], to(0, -1), F4).start()

    @pl.when(first)
    def _():
        for c in range(nc):
            got(U2, c, tb.at[6])

            @pl.when(no(low1))
            def _():
                copy(U3, c, tb.at[6], tb.at[7], to(0, 1)).start()

            @pl.when(c1)
            def _():
                copy(U1, c, tb.at[6], tb.at[5], to(0, -1)).start()

        def seam(j, carry):
            slot = jnp.where(c0, pick(j, (4, 6, 5, 7)), pick(j, (4, 5, 6, 7)))

            @pl.when(slot == 5)
            def _():
                each(lambda c: got(U1, c, tb.at[5]))

            @pl.when(both(slot == 7, no(one0)))
            def _():
                each(lambda c: got(U3, c, tb.at[7]))
            score(tb[slot], sl.at[slot, :, 0:PAD], 0, PAD)
            return carry
        lax.fori_loop(0, 4, seam, 0)
        for n in range(3):
            cols = slice(n * part, (n + 1) * part)
            gi[:, cols] += image_part(0, 4, cols)
        for c in range(nc):
            sent(U1, c, tb.at[4])
            sent(U2, c, tb.at[4])
            pl.when(no(low1))(lambda: sent(U3, c, tb.at[6]))
            pl.when(one0)(lambda: sent(F4, c, tb.at[7]))

    @pl.when(c0)
    def _():
        for c in range(nc):
            got(PA, c, ra)
            pt[0, span(c), :] += ra[span(c), :].astype(jnp.float32)

    @pl.when(six1)
    def _():
        for c in range(nc):
            got(PX, c, rx)
            pt[0, span(c), :] += rx[span(c), :].astype(jnp.float32)

    def back(c, src, norm, hat, out):
        n = norm[span(c), :]
        unit = src[span(c), :].astype(jnp.float32) / n
        along = jnp.sum(unit * hat, axis=1, keepdims=True)
        out[span(c), :] = (hat - unit * along) / n

    for c in range(nc):
        @pl.when(no(first))
        def _():
            got(GS, c, tb.at[4])
            gi[span(c), :] += tb[4, span(c), :].astype(jnp.float32)
        back(c, img_ref, inorm, gi[span(c), :], ig_ref)

    @pl.when(no(first))
    def _():
        lcopy.wait_recv()
        la[:, 0:PAD] += lr[...]
    loss_ref[...] = la[0:1, 0:rows] / (PAIRS * rows)
    for c in range(nc):
        got(QS, c, rq)
        back(c, txt_ref, tnorm, pt[0, span(c), :] + rq[span(c), :].astype(jnp.float32), tg_ref)

    for c in range(nc):
        sent(T1, c, tb.at[1])
        sent(IM, c, xs)
        sent(PB, c, s3)
        sent(GS, c, sgi)
        pl.when(high0)(lambda: sent(W2, c, tb.at[0]))
        pl.when(no(high0))(lambda: sent(T2, c, tb.at[0]))
        sent(QS, c, sq)
        pl.when(jnp.logical_or(one0, high0))(lambda: sent(F2, c, tb.at[3]))
        pl.when(no(low1))(lambda: sent(T3, c, tb.at[2]))

        pl.when(low0)(lambda: sent(PX, c, s3))
        pl.when(no(low0))(lambda: sent(PA, c, s3))

    @pl.when(no(last))
    def _():
        lcopy.wait_send()


def solution(mesh):
    n_blk, n_grp = mesh.shape["blk"], mesh.shape["grp"]

    def body(image_embed, text_embed, log_scale, logit_bias):
        rows, width = image_embed.shape
        nc = CHUNKS
        half = lambda *shape: pltpu.VMEM(shape, jnp.bfloat16)
        full = lambda *shape: pltpu.VMEM(shape, jnp.float32)
        dma = pltpu.SemaphoreType.DMA
        vmem = pl.BlockSpec(memory_space=pltpu.VMEM)
        smem = pl.BlockSpec(memory_space=pltpu.SMEM)
        out = lambda *shape: jax.ShapeDtypeStruct(shape, jnp.float32)
        image_grad, text_grad, loss = pl.pallas_call(
            functools.partial(kernel, n_blk, n_grp, nc),
            out_shape=(out(rows, width), out(rows, width), out(1, rows)),
            in_specs=[vmem, vmem, smem, smem],
            out_specs=(vmem, vmem, vmem),
            scratch_shapes=[
                half(2 * PAD, width), half(8, rows, width), half(8, rows, 2 * PAD), full(rows, width),
                full(4, rows, width), *[half(rows, width)] * 9,
                full(rows, 1), full(rows, 1), full(8, 2 * PAD), full(8, PAD), full(8, PAD),
                dma((15, nc)), dma((13, nc)), dma, dma,
            ],
            compiler_params=pltpu.CompilerParams(
                collective_id=0, has_side_effects=True, vmem_limit_bytes=40 << 20),
            cost_estimate=pl.CostEstimate(flops=48 * rows * rows * width, bytes_accessed=12 * rows * width,
                                          transcendentals=24 * rows * rows),
            name="band_loss",
        )(image_embed, text_embed, log_scale, logit_bias)
        return image_grad, text_grad, loss.reshape(rows)

    in_specs = (P(("blk", "grp"), None), P(("blk", "grp"), None), P(), P())
    out_specs = (P(("blk", "grp"), None), P(("blk", "grp"), None), P(("blk", "grp")))
    return jax.shard_map(body, mesh=mesh, in_specs=in_specs, out_specs=out_specs, check_vma=False)
```

```python
import functools

import jax
import jax.numpy as jnp
from jax import lax
from jax.experimental import pallas as pl
from jax.experimental.pallas import tpu as pltpu
from jax.sharding import PartitionSpec as P

MESH = pl.DeviceIdType.MESH
EPS = 1e-06
PAIRS = 8
PAD = 256
CHUNKS = 2
T1, T2, T3, IM, PA, PB, PX, QS, GS, U1, U2, U3, W2, F2, F4 = range(15)


def kernel(n_blk, n_grp, nc, img_ref, txt_ref, scale_ref, bias_ref, ig_ref, tg_ref, loss_ref,
           xs, tb, sl, gi, pt, ra, rb, rx, rq, s1, s3, sq, sgi, w2, inorm, tnorm, la, ls, lr,
           send_sem, recv_sem, lsend, lrecv):
    blk, grp = lax.axis_index("blk"), lax.axis_index("grp")
    core = lax.rem(grp, 2)
    rows, width = img_ref.shape
    ch = rows // nc
    part = width // 3
    both = jnp.logical_and
    no = jnp.logical_not
    half = n_grp // 2
    chip = lax.rem(grp, half) // 2
    c0, c1 = core == 0, core == 1
    low, high = chip == 0, chip == half // 2 - 1
    low0, low1, high0, high1 = both(low, c0), both(low, c1), both(high, c0), both(high, c1)
    one0, six1 = both(chip == 1, c0), both(chip == half // 2 - 2, c1)
    first, last = blk == 0, blk == n_blk - 1
    origin = both(first, grp == 0)
    near = functools.reduce(jnp.logical_or, [grp == k for k in (1, 2, half - 2, n_grp - 2, n_grp - 1)])
    near = both(first, near)
    near_blk, near_six = both(blk == 1, grp == 0), both(first, grp == n_grp - 3)

    def to(db, dg):
        return (lax.rem(blk + db + n_blk, n_blk), lax.rem(grp + dg + 2 * n_grp, n_grp))

    def span(c, base=0):
        if isinstance(c, int):
            return pl.ds(base + c * ch, ch)
        return pl.ds(pl.multiple_of(base + c * ch, 16), ch)

    def copy(stream, c, src, dst, target, send=None, at=0):
        return pltpu.make_async_remote_copy(
            src_ref=src.at[span(c)], dst_ref=dst.at[span(c, at)],
            send_sem=send_sem.at[stream if send is None else send, c], recv_sem=recv_sem.at[stream, c],
            device_id=target, device_id_type=MESH)

    def got(stream, c, dst):
        copy(stream, c, dst, dst, to(0, 1)).wait_recv()

    def sent(stream, c, src):
        copy(stream, c, src, src, to(0, 1)).wait_send()

    def each(fn):
        for c in range(nc):
            fn(c)

    barrier = pltpu.get_barrier_semaphore()

    def greet(*targets):
        for db, dg in targets:
            pl.semaphore_signal(barrier, inc=1, device_id=to(db, dg), device_id_type=MESH)

    early = no(origin)
    for step_ in (1, -1, 2, -2):
        pl.when(both(early, no(both(first, lax.rem(grp + step_ + n_grp, n_grp) == 0))))(
            functools.partial(greet, (0, step_)))
    pl.when(both(early, no(last)))(lambda: greet((1, 0)))
    pl.when(no(jnp.logical_or(first, near_blk)))(lambda: greet((-1, 0)))
    pl.when(both(early, low0))(lambda: greet((0, -3), (0, -2 - half)))
    pl.when(high0)(lambda: greet((0, half)))
    pl.when(both(high0, no(near)))(lambda: greet((0, 2 + half)))
    pl.when(both(high0, both(near, grp != half - 2)))(lambda: greet((0, 2 + half)))
    pl.when(high1)(lambda: greet((0, 3)))
    pl.when(one0)(lambda: greet((0, -3)))
    pl.when(both(six1, no(near_six)))(lambda: greet((0, 3)))

    def normalize(src, norm, dst):
        def chunk(c, carry):
            r = pl.ds(pl.multiple_of(c * 32, 32), 32)
            v = src[r, :].astype(jnp.float32)
            n = jnp.sqrt(jnp.sum(v * v, axis=1, keepdims=True) + EPS)
            norm[r, :] = n
            dst[r, :] = (v / n).astype(jnp.bfloat16)
            return carry
        lax.fori_loop(0, rows // 32, chunk, 0)

    def enter():
        extra = jnp.where(jnp.logical_or(low0, high0), 2, jnp.where(jnp.logical_or(high1, jnp.logical_or(one0, six1)), 1, 0))
        fewer = jnp.where(jnp.logical_or(near, jnp.logical_or(near_blk, near_six)), 1, 0)
        pl.semaphore_wait(barrier, jnp.where(first, 5, 6) + extra - fewer)
        pl.when(first)(lambda: greet((-1, 0)))
        pl.when(last)(lambda: greet((1, 0)))
        pl.when(jnp.logical_or(near, near_six))(lambda: greet((0, n_grp - grp)))
        pl.when(near_blk)(lambda: greet((-1, 0)))
        pl.when(origin)(lambda: greet((0, 1), (0, -1), (0, 2), (0, -2), (0, half - 2), (1, 0)))

    pl.when(origin)(enter)
    normalize(txt_ref, tnorm, tb.at[0])
    normalize(img_ref, inorm, xs)
    xs[rows:PAD, :] = jnp.zeros((PAD - rows, width), jnp.bfloat16)
    xs[PAD + rows:, :] = jnp.zeros((PAD - rows, width), jnp.bfloat16)
    pl.when(no(origin))(enter)

    @pl.when(high0)
    def _():
        each(lambda c: copy(W2, c, tb.at[0], w2, to(0, half)).start())

    @pl.when(high1)
    def _():
        each(lambda c: copy(T3, c, tb.at[0], tb.at[3], to(0, 3), T2).start())

    @pl.when(no(high))
    def _():
        each(lambda c: copy(T2, c, tb.at[0], tb.at[2], to(0, 2)).start())

    def send_images():
        each(lambda c: copy(IM, c, xs, xs, to(-1, 0), at=PAD).start())

    def late_images():
        pl.semaphore_wait(barrier, jnp.where(near, 2, 1))
        send_images()

    pl.when(no(jnp.logical_or(first, near_blk)))(send_images)

    @pl.when(c0)
    def _():
        each(lambda c: copy(T1, c, tb.at[0], tb.at[1], to(0, 1)).start())

    def send_seam(c):
        copy(GS, c, tb.at[0], tb.at[4], to(1, 0)).start()

    pl.when(both(last, low))(lambda: send_seam(0))
    pl.when(both(last, no(low)))(lambda: each(send_seam))

    factor = jnp.exp(jnp.full((1, 1), scale_ref[0], jnp.float32))
    bias = bias_ref[0]
    la[...] = jnp.zeros_like(la)

    def score(text, out, lo, hi, diagonal=False):
        logit = lax.dot_general(text, xs[lo:hi, :], (((1,), (1,)), ((), ())), preferred_element_type=jnp.float32)
        x = factor * logit + bias
        minus = 1.0
        if diagonal:
            at = lax.broadcasted_iota(jnp.int32, x.shape, 0)
            to_ = lax.broadcasted_iota(jnp.int32, x.shape, 1)
            minus = jnp.where(at == to_, -1.0, 1.0).astype(jnp.float32)
            x = minus * x
        e = jnp.exp(-jnp.abs(x))
        la[0:1, lo:hi] += jnp.sum(jnp.maximum(x, 0.0) + jnp.log1p(e), axis=0, keepdims=True)
        slope = factor * minus * (jnp.where(x >= 0, 1.0, e) / (1.0 + e))
        out[...] = slope.astype(jnp.bfloat16)

    def text_part(slot, r):
        for n in range(3):
            cols = slice(n * part, (n + 1) * part)
            pt[slot, r, cols] = jnp.dot(sl[slot, r, :], xs[:, cols], preferred_element_type=jnp.float32)

    def image_part(lo, slot, cols):
        return lax.dot_general(
            sl[slot:slot + 4, :, lo:lo + rows].reshape(4 * rows, rows), tb[slot:slot + 4, :, cols].reshape(4 * rows, part),
            (((0,), (0,)), ((), ())), preferred_element_type=jnp.float32)

    def arrive2(c):
        got(T2, c, tb.at[2])

        @pl.when(no(jnp.logical_or(low1, both(near, high1))))
        def _():
            copy(T3, c, tb.at[2], tb.at[3], to(0, 1)).start()

        @pl.when(c1)
        def _():
            copy(T1, c, tb.at[2], tb.at[1], to(0, -1)).start()

    def arrive3(c):
        got(T3, c, tb.at[3])

        @pl.when(one0)
        def _():
            copy(T2, c, tb.at[3], tb.at[2], to(0, -1), F2).start()

    def seam_chunk(c):
        got(GS, c, tb.at[4])

        @pl.when(high1)
        def _():
            copy(U3, c, tb.at[4], tb.at[7], to(0, 3), U2).start()

        @pl.when(no(high1))
        def _():
            copy(U2, c, tb.at[4], tb.at[6], to(0, 2)).start()

        @pl.when(c0)
        def _():
            copy(U1, c, tb.at[4], tb.at[5], to(0, 1)).start()

    def seam_start():
        each(seam_chunk)

    every = pl.ds(0, rows)
    score(tb[0], sl.at[0, :, 0:PAD], 0, PAD, True)
    pl.when(no(low))(lambda: each(arrive2))

    def relay():
        for c in range(nc):
            got(W2, c, w2)
            copy(T2, c, w2, tb.at[2], to(0, 2 + half), F2).start()

    before_origin = both(first, grp == half - 2)
    pl.when(both(high0, no(before_origin)))(relay)
    pl.when(one0)(lambda: each(arrive3))
    pl.when(jnp.logical_or(both(near, low), near_blk))(late_images)
    got(IM, 0, xs)

    @pl.when(both(last, low))
    def _():
        for c in range(1, nc):
            send_seam(c)
    for c in range(1, nc):
        got(IM, c, xs)

    pl.when(both(first, no(low)))(late_images)
    pl.when(before_origin)(relay)

    @pl.when(both(high1, near))
    def _():
        each(lambda c: copy(T3, c, tb.at[2], tb.at[3], to(0, 1)).start())

    def pick(j, values):
        out = jnp.int32(values[-1])
        for i in range(len(values) - 1):
            out = jnp.where(j == i, values[i], out)
        return out

    def combine(c):
        got(PB, c, rb)
        sq[span(c), :] = (pt[2, span(c), :] + rb[span(c), :].astype(jnp.float32)).astype(jnp.bfloat16)
        copy(QS, c, sq, rq, to(0, -2)).start()

    def meet(slot, r, chunks):
        @pl.when(slot == 1)
        def _():
            for c in chunks:
                got(T1, c, tb.at[1])

        @pl.when(both(slot == 3, no(one0)))
        def _():
            for c in chunks:
                arrive3(c)
        score(tb[slot, r, :], sl.at[slot, r, :], 0, 2 * PAD)
        text_part(slot, r)

        @pl.when(slot == 1)
        def _():
            for c in chunks:
                s1[span(c), :] = pt[1, span(c), :].astype(jnp.bfloat16)
                pl.when(c0)(lambda: copy(PB, c, s1, rb, to(0, 1)).start())
                pl.when(c1)(lambda: copy(PA, c, s1, ra, to(0, -1)).start())

        @pl.when(slot == 3)
        def _():
            for c in chunks:
                s3[span(c), :] = pt[3, span(c), :].astype(jnp.bfloat16)
                pl.when(low0)(lambda: copy(PX, c, s3, rx, to(0, -3)).start())
                pl.when(both(c0, no(low)))(lambda: copy(PA, c, s3, ra, to(0, -1)).start())
                pl.when(c1)(lambda: copy(PB, c, s3, rb, to(0, -1)).start())

        @pl.when(both(c0, jnp.where(low, slot == 1, slot == 2)))
        def _():
            for c in chunks:
                combine(c)

    def score_own():
        score(tb[0], sl.at[0, :, PAD:], PAD, 2 * PAD)

    pl.when(low)(score_own)

    @pl.when(low)
    def _():
        def step(j, carry):
            slot = jnp.where(c0, pick(lax.rem(j, 3), (2, 3, 1)),
                             jnp.where(j < nc, 1, jnp.where(lax.rem(j - nc, 2) == 0, 3, 2)))
            c = jnp.where(c0, j // 3, jnp.where(j < nc, j, (j - nc) // 2))

            @pl.when(jnp.where(c0, slot == 2, slot == 3))
            def _():
                arrive2(c)
            meet(slot, span(c), (c,))
            pl.when(both(both(first, no(near)), j == 1))(late_images)

            for k in range(nc):
                pl.when(both(first, j == 2 + 3 * k))(functools.partial(seam_chunk, k))
            return carry
        lax.fori_loop(0, 3 * nc, step, 0)

    @pl.when(no(low))
    def _():
        def step(j, carry):
            meet(jnp.where(c0, pick(j, (2, 1, 3)), pick(j, (3, 2, 1))), every, range(nc))
            return carry
        lax.fori_loop(0, 3, step, 0)

    pl.when(no(low))(score_own)
    ls[...] = la[:, PAD:]
    lcopy = pltpu.make_async_remote_copy(src_ref=ls, dst_ref=lr, send_sem=lsend, recv_sem=lrecv,
                                         device_id=to(1, 0), device_id_type=MESH)

    @pl.when(no(last))
    def _():
        lcopy.start()
        for n in range(3):
            cols = slice(n * part, (n + 1) * part)
            sgi[:, cols] = image_part(PAD, 0, cols).astype(jnp.bfloat16)
        each(lambda c: copy(GS, c, sgi, tb.at[4], to(1, 0)).start())

    text_part(0, every)
    for n in range(3):
        cols = slice(n * part, (n + 1) * part)
        gi[:, cols] = image_part(0, 0, cols)

    pl.when(both(first, no(low)))(seam_start)

    @pl.when(c1)
    def _():
        for c in range(nc):
            got(PB, c, rb)
            pt[2, span(c), :] += rb[span(c), :].astype(jnp.float32)

            @pl.when(no(high))
            def _():
                got(PA, c, ra)
                pt[2, span(c), :] += ra[span(c), :].astype(jnp.float32)
            sq[span(c), :] = pt[2, span(c), :].astype(jnp.bfloat16)
            copy(QS, c, sq, rq, to(0, -2)).start()

    @pl.when(both(first, one0))
    def _():
        for c in range(nc):
            got(U3, c, tb.at[7])
            copy(U2, c, tb.at[7], tb.at[6], to(0, -1), F4).start()

    @pl.when(first)
    def _():
        for c in range(nc):
            got(U2, c, tb.at[6])

            @pl.when(no(low1))
            def _():
                copy(U3, c, tb.at[6], tb.at[7], to(0, 1)).start()

            @pl.when(c1)
            def _():
                copy(U1, c, tb.at[6], tb.at[5], to(0, -1)).start()

        def seam(j, carry):
            slot = jnp.where(c0, pick(j, (4, 6, 5, 7)), pick(j, (4, 5, 6, 7)))

            @pl.when(slot == 5)
            def _():
                each(lambda c: got(U1, c, tb.at[5]))

            @pl.when(both(slot == 7, no(one0)))
            def _():
                each(lambda c: got(U3, c, tb.at[7]))
            score(tb[slot], sl.at[slot, :, 0:PAD], 0, PAD)
            return carry
        lax.fori_loop(0, 4, seam, 0)
        for n in range(3):
            cols = slice(n * part, (n + 1) * part)
            gi[:, cols] += image_part(0, 4, cols)
        for c in range(nc):
            sent(U1, c, tb.at[4])
            sent(U2, c, tb.at[4])
            pl.when(no(low1))(lambda: sent(U3, c, tb.at[6]))
            pl.when(one0)(lambda: sent(F4, c, tb.at[7]))

    @pl.when(c0)
    def _():
        for c in range(nc):
            got(PA, c, ra)
            pt[0, span(c), :] += ra[span(c), :].astype(jnp.float32)

    @pl.when(six1)
    def _():
        for c in range(nc):
            got(PX, c, rx)
            pt[0, span(c), :] += rx[span(c), :].astype(jnp.float32)

    def back(c, src, norm, hat, out):
        n = norm[span(c), :]
        unit = src[span(c), :].astype(jnp.float32) / n
        along = jnp.sum(unit * hat, axis=1, keepdims=True)
        out[span(c), :] = (hat - unit * along) / n

    for c in range(nc):
        @pl.when(no(first))
        def _():
            got(GS, c, tb.at[4])
            gi[span(c), :] += tb[4, span(c), :].astype(jnp.float32)
        back(c, img_ref, inorm, gi[span(c), :], ig_ref)

    @pl.when(no(first))
    def _():
        lcopy.wait_recv()
        la[:, 0:PAD] += lr[...]
    loss_ref[...] = la[0:1, 0:rows] / (PAIRS * rows)
    for c in range(nc):
        got(QS, c, rq)
        back(c, txt_ref, tnorm, pt[0, span(c), :] + rq[span(c), :].astype(jnp.float32), tg_ref)

    for c in range(nc):
        sent(T1, c, tb.at[1])
        sent(IM, c, xs)
        sent(PB, c, s3)
        sent(GS, c, sgi)
        pl.when(high0)(lambda: sent(W2, c, tb.at[0]))
        pl.when(no(high0))(lambda: sent(T2, c, tb.at[0]))
        sent(QS, c, sq)
        pl.when(jnp.logical_or(one0, high0))(lambda: sent(F2, c, tb.at[3]))
        pl.when(no(low1))(lambda: sent(T3, c, tb.at[2]))

        pl.when(low0)(lambda: sent(PX, c, s3))
        pl.when(no(low0))(lambda: sent(PA, c, s3))

    @pl.when(no(last))
    def _():
        lcopy.wait_send()


def solution(mesh):
    n_blk, n_grp = mesh.shape["blk"], mesh.shape["grp"]

    def body(image_embed, text_embed, log_scale, logit_bias):
        rows, width = image_embed.shape
        nc = CHUNKS
        half = lambda *shape: pltpu.VMEM(shape, jnp.bfloat16)
        full = lambda *shape: pltpu.VMEM(shape, jnp.float32)
        dma = pltpu.SemaphoreType.DMA
        vmem = pl.BlockSpec(memory_space=pltpu.VMEM)
        smem = pl.BlockSpec(memory_space=pltpu.SMEM)
        out = lambda *shape: jax.ShapeDtypeStruct(shape, jnp.float32)
        image_grad, text_grad, loss = pl.pallas_call(
            functools.partial(kernel, n_blk, n_grp, nc),
            out_shape=(out(rows, width), out(rows, width), out(1, rows)),
            in_specs=[vmem, vmem, smem, smem],
            out_specs=(vmem, vmem, vmem),
            scratch_shapes=[
                half(2 * PAD, width), half(8, rows, width), half(8, rows, 2 * PAD), full(rows, width),
                full(4, rows, width), *[half(rows, width)] * 9,
                full(rows, 1), full(rows, 1), full(8, 2 * PAD), full(8, PAD), full(8, PAD),
                dma((15, nc)), dma((13, nc)), dma, dma,
            ],
            compiler_params=pltpu.CompilerParams(
                collective_id=0, has_side_effects=True, vmem_limit_bytes=40 << 20),
            cost_estimate=pl.CostEstimate(flops=48 * rows * rows * width, bytes_accessed=12 * rows * width,
                                          transcendentals=24 * rows * rows),
            name="band_loss",
        )(image_embed, text_embed, log_scale, logit_bias)
        return image_grad, text_grad, loss.reshape(rows)

    in_specs = (P(("blk", "grp"), None), P(("blk", "grp"), None), P(), P())
    out_specs = (P(("blk", "grp"), None), P(("blk", "grp"), None), P(("blk", "grp")))
    return jax.shard_map(body, mesh=mesh, in_specs=in_specs, out_specs=out_specs, check_vma=False)
```
